32 devices in a mesh: groups: 2 (over y), dict: 16 (over z, x, core).
Axes of the slice: x: 2, y: 2, z: 4, core: 2. Of those that a mesh axis runs over, the one named last changes fastest.
Arguments:
- activations: bfloat16 [4096, 3584], P(('groups', 'dict')), parts along dimension 0, may hold values from -6 to 6
- block_ids: int32 [4096, 32], P(('groups', 'dict')), parts along dimension 0, may hold values from 0 to 63, as said below
- slot_mask: int32 [4096, 32], P(('groups', 'dict')), parts along dimension 0, may hold values from 0 to 1
- enc_weight: bfloat16 [3584, 4096], P(None, 'dict'), may hold values from -0.09375 to 0.09375
- enc_bias: float32 [4096], P('dict'), may hold values from -3 to 3
- dec_weight: bfloat16 [4096, 3584], P('dict'), may hold values from -0.75 to 0.75
- dec_bias: float32 [3584], replicated, may hold values from -3 to 3
Outputs:
- recon_error: bfloat16 [4096, 3584], P(('groups', 'dict')), parts along dimension 0
- grad_enc: float32 [7168, 4096], P('groups', 'dict'), parts along dimension 0
- grad_enc_bias: float32 [8192], P(('groups', 'dict')), parts along dimension 0
- grad_dec: float32 [8192, 3584], P(('groups', 'dict')), parts along dimension 0
- grad_dec_bias: float32 [7168], P('groups'), parts along dimension 0
The draws below stay inside these ranges and needn't reach their ends.
There are 2 independent parts, one for each index of `groups`. The reference program is written for one: setup_inputs(seed, part) draws one part's arguments, and reference() takes and returns one part's arrays. A program takes and returns all parts, laid end to end along the dimension named above; an argument that names none is the same for every part. Nothing has to cross between parts.
Inputs may be any that keep to these rules, and one draw needn't show every extreme that they name: `block_ids`: slot k of a row names one of the blocks k * 2 to (k + 1) * 2 - 1, so a row's blocks are distinct. Among the rows of one device (aligned blocks of 128 rows) each block is named by at most 2 live slots, and in every draw some block is named by exactly 2 live slots on every device. Slots that are not live carry nothing.
All inputs are finite; a program needn't handle non-finite values.
Results may differ from the reference program's by a relative error of at most 0.0049.
Values may be sent and summed in bfloat16 or wider, within the bound.
A program may use at most 128 MiB of HBM per device.

```python
import jax
import jax.numpy as jnp
from jax import lax

D = 3584
BLOCK = 64
SLOTS = 32
CAP = 2
ROW_DEV = 128
NBLK = 64
ROWS = 2048


def routing(key):
    device_count = ROWS // ROW_DEV
    per_group = NBLK // SLOTS
    key_popular, key_counts, key_star, key_places = jax.random.split(key, 4)
    popular = jax.random.randint(key_popular, (NBLK,), 0, 4) == 0
    ceiling = jnp.where(popular, CAP, 1)
    counts = jax.random.randint(key_counts, (device_count, NBLK), 0, CAP + 1)
    counts = jnp.minimum(counts, ceiling[None, :])
    star_block = jax.random.randint(key_star, (), 0, NBLK)
    counts = jnp.where(jnp.arange(NBLK)[None, :] == star_block, CAP, counts)
    counts = counts.reshape(device_count, SLOTS, per_group)
    bounds = jnp.cumsum(counts, axis=2)
    place_keys = jax.random.split(key_places, device_count * SLOTS)
    places = jax.vmap(lambda subkey: jax.random.permutation(subkey, ROW_DEV))(place_keys)
    places = places.reshape(device_count, SLOTS, ROW_DEV)
    chosen = jnp.sum((bounds[:, :, :, None] <= places[:, :, None, :]).astype(jnp.int32), axis=2)
    is_live = places < bounds[:, :, -1:]
    within = jnp.where(is_live, jnp.minimum(chosen, per_group - 1), places % per_group)
    column = jnp.arange(SLOTS, dtype=jnp.int32)[None, :, None]
    block_list = column * per_group + within
    block_list = block_list.transpose(0, 2, 1).reshape(ROWS, SLOTS).astype(jnp.int32)
    live_list = is_live.transpose(0, 2, 1).reshape(ROWS, SLOTS).astype(jnp.int32)
    return (block_list, live_list)


def draw_block_ids(key, part):
    return routing(key)[0]


def draw_slot_mask(key, part):
    return routing(key)[1]


def steps_of(own_key, dims, shards, least, top_value):
    gain, own = 1.0, jax.random.fold_in(own_key, 6)
    for position, shards_of in shards:
        steps = jnp.exp(jax.random.uniform(jax.random.fold_in(own, position), (shards_of,), jnp.float32, least / len(shards), top_value / len(shards)))
        gain = gain * jnp.repeat(steps, dims[position] // shards_of).reshape([-1 if axis == position else 1 for axis in range(len(dims))])
    return gain


def bell_draw(rng, shape, spread, limit, cuts=(), kind=jnp.bfloat16):
    factor_of = steps_of(rng, shape, cuts, -0.22, 0.18) if cuts else 1.0
    result = jax.random.normal(rng, shape, jnp.float32) * spread * factor_of
    return jnp.minimum(jnp.maximum(result, -limit), limit).astype(kind)


def setup_inputs(seed: int = 0, part: int = 0) -> dict:
    arg_keys = jax.random.split(jax.random.key(seed), 8)
    part_splits = jax.random.split(jax.random.fold_in(arg_keys[7], part), 8)
    return {
        "activations": bell_draw(part_splits[0], (ROWS, D), 1.0, 6.0, ((0, 16),)),
        "block_ids": draw_block_ids(jax.random.fold_in(jax.random.fold_in(arg_keys[7], part), 71), part),
        "slot_mask": draw_slot_mask(jax.random.fold_in(jax.random.fold_in(arg_keys[7], part), 71), part),
        "enc_weight": bell_draw(arg_keys[3], (D, NBLK * BLOCK), D ** -0.5, 0.09375, ((1, 16),)),
        "enc_bias": bell_draw(arg_keys[4], (NBLK * BLOCK,), 0.5, 3.0, ((0, 16),), jnp.float32),
        "dec_weight": bell_draw(arg_keys[5], (NBLK * BLOCK, D), BLOCK ** -0.5, 0.75, ((0, 16),)),
        "dec_bias": bell_draw(arg_keys[6], (D,), 0.5, 3.0, (), jnp.float32),
    }


def reference(activations, block_ids, slot_mask, enc_weight, enc_bias, dec_weight, dec_bias):
    norm_scale = 1.0 / ROW_DEV
    capacity = CAP * (ROWS // ROW_DEV)
    is_live = slot_mask == 1
    block_list = jnp.arange(NBLK, dtype=jnp.int32)

    def gather_rows(block_index):
        row_hits = jnp.any((block_ids == block_index) & is_live, axis=1)
        hit_count = jnp.sum(row_hits.astype(jnp.int32))
        picked = jnp.nonzero(row_hits, size=capacity, fill_value=0)[0].astype(jnp.int32)
        in_use = jnp.arange(capacity, dtype=jnp.int32) < hit_count
        return picked, in_use

    def encode(block_index, chosen_rows, in_use):
        start = block_index * BLOCK
        weight_block = lax.dynamic_slice_in_dim(enc_weight, start, BLOCK, 1)
        bias_block = lax.dynamic_slice_in_dim(enc_bias, start, BLOCK, 0)
        preact = jnp.dot(chosen_rows, weight_block, preferred_element_type=jnp.float32) + bias_block[None, :]
        return jnp.where(in_use[:, None], jnp.maximum(preact, 0.0), 0.0).astype(jnp.bfloat16)

    def add_block(summed, block_index):
        picked, in_use = gather_rows(block_index)
        chosen_rows = activations[picked]
        latent = encode(block_index, chosen_rows, in_use)
        dec_block = lax.dynamic_slice_in_dim(dec_weight, block_index * BLOCK, BLOCK, 0)
        partial_terms = jnp.dot(latent, dec_block, preferred_element_type=jnp.float32).astype(jnp.bfloat16)
        partial_terms = lax.optimization_barrier(partial_terms).astype(jnp.float32)
        partial_terms = jnp.where(in_use[:, None], partial_terms, 0.0)
        return summed.at[picked].add(partial_terms), None

    summed = lax.scan(add_block, jnp.zeros((ROWS, D), jnp.float32), block_list)[0]
    residual = summed + dec_bias[None, :] - activations.astype(jnp.float32)
    recon_error = residual.astype(jnp.bfloat16)
    grad_dec_bias = norm_scale * jnp.sum(residual, axis=0)

    def block_grads(block_index):
        picked, in_use = gather_rows(block_index)
        chosen_rows = activations[picked]
        error_rows = recon_error[picked]
        latent = encode(block_index, chosen_rows, in_use)
        dec_block = lax.dynamic_slice_in_dim(dec_weight, block_index * BLOCK, BLOCK, 0)
        grad_dec_block = norm_scale * jnp.dot(latent.T, error_rows, preferred_element_type=jnp.float32)
        dlatent = norm_scale * jnp.dot(error_rows, dec_block.T, preferred_element_type=jnp.float32)
        dlatent = jnp.where(latent > 0, dlatent, 0.0)
        grad_bias_block = jnp.sum(dlatent, axis=0)
        grad_enc_block = jnp.dot(chosen_rows.T, dlatent.astype(jnp.bfloat16), preferred_element_type=jnp.float32)
        return grad_enc_block, grad_bias_block, grad_dec_block

    enc_parts, bias_parts, dec_parts = lax.map(block_grads, block_list)
    grad_enc = enc_parts.transpose(1, 0, 2).reshape(D, NBLK * BLOCK)
    grad_enc_bias = bias_parts.reshape(NBLK * BLOCK)
    grad_dec = dec_parts.reshape(NBLK * BLOCK, D)
    return recon_error, grad_enc, grad_enc_bias, grad_dec, grad_dec_bias
```

```python
import functools

import jax
import jax.numpy as jnp
from jax import lax
from jax.experimental import pallas as pl
from jax.experimental.pallas import tpu as pltpu
from jax.sharding import PartitionSpec as P

BLOCK = 64
CAP = 2
ROW_DEV = 128
SCALE = 1.0 / ROW_DEV
LANES = 128
VMEM_LIMIT = 58 * 1024 * 1024
F32 = jnp.float32
BF16 = jnp.bfloat16


def chunk_list(half):
    units = half // LANES
    parts = [4, 4, 4] if units > 12 else []
    rest = units - sum(parts)
    parts = ([rest] if rest else []) + parts
    out, start = [], 0
    for part in parts:
        out.append((start * LANES, part * LANES))
        start += part
    return out


def dot(a, b):
    return jnp.dot(a, b, preferred_element_type=F32)


def dot_nt(a, b):
    return lax.dot_general(a, b, (((1,), (1,)), ((), ())), preferred_element_type=F32)


def dot_tn(a, b):
    return lax.dot_general(a, b, (((0,), (0,)), ((), ())), preferred_element_type=F32)


def exchange_kernel(
    n, slots, ids_ref, live_ref, act_ref, enc_bias_ref, dec_bias_ref, enc_hbm, dec_hbm,
    recon_ref, rows_hbm, err_hbm, lat_ref, dlat_ref, enc_grad_ref, sum_ref,
    enc, dec, out_buf, rows_in, term_out, term_in, err_in, pick, pick_t, part, part_in,
    load_sem, store_sem, send1, recv1, send2, recv2, send3, recv3, send4, recv4,
):
    me = lax.axis_index("dict")
    rows_total = 16 * n
    rows = act_ref.shape[0]
    half = act_ref.shape[1] // 2
    width = BLOCK * 4
    chunks = chunk_list(half)
    bits = [1 << k for k in range(n.bit_length() - 1)]

    def peer_of(step):
        index = n - step
        return sum(((me // bit + index // bit) % 2) * bit for bit in bits)

    def for_peers(fn):
        def step_fn(step, carry):
            fn(peer_of(step))
            return carry

        lax.fori_loop(1, n, step_fn, 0)

    barrier = pltpu.get_barrier_semaphore()
    for_peers(
        lambda peer: pl.semaphore_signal(
            barrier, inc=1, device_id={"dict": peer}, device_id_type=pl.DeviceIdType.MESH
        )
    )
    enc_load = pltpu.make_async_copy(enc_hbm, enc, load_sem.at[0])
    dec_load = pltpu.make_async_copy(dec_hbm, dec, load_sem.at[1])
    enc_load.start()
    dec_load.start()

    def block_rows(device):
        return pl.ds(pl.multiple_of(device * 16, 16), 16)

    def send(src, dst, start, size, send_sem, recv_sem):
        mine = block_rows(me)
        columns = pl.ds(start, size)

        def one(peer):
            pltpu.make_async_remote_copy(
                src_ref=src.at[block_rows(peer), columns],
                dst_ref=dst.at[mine, columns],
                send_sem=send_sem,
                recv_sem=recv_sem,
                device_id={"dict": peer},
                device_id_type=pl.DeviceIdType.MESH,
            ).start()

        for_peers(one)
        dst[mine, columns] = src[mine, columns]

    def wait_all(buf, start, size, sem):
        view = buf.at[pl.ds(0, (n - 1) * 16), pl.ds(start, size)]
        pltpu.make_async_copy(view, view, sem).wait()

    column = lax.broadcasted_iota(jnp.int32, (slots, rows_total), 1)
    block = (column // 16) * 4 + (column % 8) // CAP
    per_slot = 4 * n // slots
    spread = (
        lax.broadcasted_iota(jnp.int32, (slots, rows_total), 0) == block // per_slot
    ).astype(F32).astype(BF16)
    slot_base = lax.broadcasted_iota(jnp.int32, (rows, slots), 1) * per_slot
    code = jnp.where(live_ref[...] == 1, ids_ref[...] - slot_base + 1, 0).astype(F32)
    code = dot(code.astype(BF16), spread)
    column = lax.broadcasted_iota(jnp.int32, (rows, rows_total), 1)
    block = (column // 16) * 4 + (column % 8) // CAP
    hit = code == (block % per_slot + 1).astype(F32)
    lower = (
        lax.broadcasted_iota(jnp.int32, (rows, rows), 1)
        < lax.broadcasted_iota(jnp.int32, (rows, rows), 0)
    ).astype(F32).astype(BF16)
    earlier = dot(lower, hit.astype(F32).astype(BF16))
    chosen = hit & (earlier == (column % CAP).astype(F32))
    top = (column // 8) % 2
    pick_low = jnp.where(chosen & (top == 0), 1.0, 0.0)
    pick_high = jnp.where(chosen & (top == 1), 1.0, 0.0)
    both = jnp.concatenate([pick_low, pick_high], axis=0)
    pick[...] = both.astype(BF16)
    pick_t[...] = both.T.astype(BF16)

    for start, size in chunks:
        stacked = jnp.concatenate(
            [act_ref[:, start : start + size], act_ref[:, half + start : half + start + size]],
            axis=0,
        )
        out_buf[:, start : start + size] = dot(pick_t[...], stacked).astype(BF16)

    pl.semaphore_wait(barrier, n - 1)
    send(out_buf, rows_in, 0, half, send1, recv1)
    enc_load.wait()
    wait_all(rows_in, 0, half, recv1)

    low = dot(rows_in[...], enc[:half, :]).reshape(n, 2, 8, width)
    high = dot(rows_in[...], enc[half:, :]).reshape(n, 2, 8, width)
    preact = low[:, 0] + high[:, 1] + enc_bias_ref[...].reshape(1, 1, width)
    own_block = (
        lax.broadcasted_iota(jnp.int32, (n, 8, width), 1) // CAP
        == lax.broadcasted_iota(jnp.int32, (n, 8, width), 2) // BLOCK
    )
    latent = jnp.where(own_block, jnp.maximum(preact, 0.0), 0.0)

    def stack(value):
        value = jnp.broadcast_to(value[:, None], (n, 2, 8, width))
        return value.reshape(rows_total, width)

    latent_both = stack(latent)
    lat_ref[...] = latent_both.astype(BF16)
    live_top = (lax.broadcasted_iota(jnp.int32, (rows_total, width), 0) // 8) % 2
    latent_low = jnp.where(live_top == 0, latent_both, 0.0).astype(BF16)
    latent_high = jnp.where(live_top == 1, latent_both, 0.0).astype(BF16)

    dec_load.wait()
    for c, (start, size) in enumerate(chunks):
        value = dot(latent_low, dec[:, start : start + size])
        value = value + dot(latent_high, dec[:, half + start : half + start + size])
        term_out[:, start : start + size] = value.astype(BF16)
        send(term_out, term_in, start, size, send2.at[c], recv2.at[c])

    rows_store = pltpu.make_async_copy(rows_in, rows_hbm, store_sem.at[0])
    rows_store.start()
    wait_all(out_buf, 0, half, send1)

    units_per = part.shape[1]
    part[...] = jnp.zeros_like(part)
    for c, (start, size) in enumerate(chunks):
        wait_all(term_in, start, size, recv2.at[c])
        combined = dot(pick[...], term_in[:, start : start + size])
        errors = []
        for h in range(2):
            first = h * half + start
            residual = combined[h * rows : (h + 1) * rows]
            residual = residual + dec_bias_ref[:, first : first + size]
            residual = residual - act_ref[:, first : first + size].astype(F32)
            error = residual.astype(BF16)
            recon_ref[:, first : first + size] = error
            errors.append(error)
            total = SCALE * jnp.sum(residual, axis=0, keepdims=True)
            for u in range(size // LANES):
                unit = first // LANES + u
                part[unit // units_per, unit % units_per, :] = total[
                    0, u * LANES : (u + 1) * LANES
                ]
        out_buf[:, start : start + size] = dot(
            pick_t[...], jnp.concatenate(errors, axis=0)
        ).astype(BF16)
        send(out_buf, err_in, start, size, send3.at[c], recv3.at[c])

    def send_part(peer):
        pltpu.make_async_remote_copy(
            src_ref=part.at[peer],
            dst_ref=part_in.at[me],
            send_sem=send4.at[0],
            recv_sem=recv4.at[0],
            device_id={"dict": peer},
            device_id_type=pl.DeviceIdType.MESH,
        ).start()

    for_peers(send_part)
    part_in[me] = part[me]

    def wait_parts(buf, sem):
        view = buf.at[pl.ds(0, n - 1)]
        pltpu.make_async_copy(view, view, sem).wait()

    wait_parts(part_in, recv4.at[0])
    wait_parts(part, send4.at[0])
    sum_ref[me] = jnp.sum(part_in[...], axis=0)

    def send_total(peer):
        pltpu.make_async_remote_copy(
            src_ref=sum_ref.at[me],
            dst_ref=sum_ref.at[me],
            send_sem=send4.at[1],
            recv_sem=recv4.at[1],
            device_id={"dict": peer},
            device_id_type=pl.DeviceIdType.MESH,
        ).start()

    for_peers(send_total)

    low = jnp.zeros((rows_total, width), F32)
    high = jnp.zeros((rows_total, width), F32)
    stores = []
    for c, (start, size) in enumerate(chunks):
        wait_all(err_in, start, size, recv3.at[c])
        columns = pl.ds(start, size)
        store = pltpu.make_async_copy(
            err_in.at[:, columns], err_hbm.at[:, columns], store_sem.at[1 + c]
        )
        store.start()
        stores.append(store)
        value = err_in[:, start : start + size]
        low = low + dot_nt(value, dec[:, start : start + size])
        high = high + dot_nt(value, dec[:, half + start : half + start + size])
    low = low.reshape(n, 2, 8, width)
    high = high.reshape(n, 2, 8, width)
    latent = lat_ref[...].astype(F32).reshape(n, 2, 8, width)[:, 0]
    dlatent = jnp.where(latent > 0, SCALE * (low[:, 0] + high[:, 1]), 0.0)
    enc_grad_ref[...] = jnp.sum(dlatent.reshape(n * 8, width), axis=0, keepdims=True)
    dlat_ref[...] = stack(dlatent).astype(BF16)

    for c, (start, size) in enumerate(chunks):
        wait_all(term_out, start, size, send2.at[c])
        wait_all(out_buf, start, size, send3.at[c])
        stores[c].wait()
    rows_store.wait()
    wait_parts(sum_ref, recv4.at[1])
    wait_parts(sum_ref, send4.at[1])


def grad_kernel(rows_ref, err_ref, lat_ref, dlat_ref, enc_ref, dec_ref):
    h = pl.program_id(0)
    top = (lax.broadcasted_iota(jnp.int32, lat_ref.shape, 0) // 8) % 2
    keep = top == h
    latent = jnp.where(keep, lat_ref[...].astype(F32), 0.0).astype(BF16)
    dlatent = jnp.where(keep, dlat_ref[...].astype(F32), 0.0).astype(BF16)
    enc_ref[...] = dot_tn(rows_ref[...], dlatent)
    dec_ref[...] = SCALE * dot_tn(latent, err_ref[...])


def body(activations, block_ids, slot_mask, enc_weight, enc_bias, dec_weight, dec_bias):
    n = lax.axis_size("dict")
    rows, model_width = activations.shape
    half = model_width // 2
    width = enc_bias.shape[0]
    rows_total = 16 * n
    units = model_width // LANES
    units_per = -(-units // n)
    chunks = len(chunk_list(half))
    vmem = pl.BlockSpec(memory_space=pltpu.VMEM)
    hbm = pl.BlockSpec(memory_space=pl.ANY)
    slot_buf = pltpu.VMEM((rows_total, half), BF16)
    recon_error, rows_in, err_in, latent, dlatent, enc_bias_grad, sums = pl.pallas_call(
        functools.partial(exchange_kernel, n, block_ids.shape[1]),
        out_shape=(
            jax.ShapeDtypeStruct((rows, model_width), BF16),
            jax.ShapeDtypeStruct((rows_total, half), BF16),
            jax.ShapeDtypeStruct((rows_total, half), BF16),
            jax.ShapeDtypeStruct((rows_total, width), BF16),
            jax.ShapeDtypeStruct((rows_total, width), BF16),
            jax.ShapeDtypeStruct((1, width), F32),
            jax.ShapeDtypeStruct((n, units_per, LANES), F32),
        ),
        in_specs=[vmem] * 5 + [hbm] * 2,
        out_specs=(vmem, hbm, hbm, vmem, vmem, vmem, vmem),
        scratch_shapes=[
            pltpu.VMEM((model_width, width), BF16),
            pltpu.VMEM((width, model_width), BF16),
            slot_buf,
            slot_buf,
            slot_buf,
            slot_buf,
            slot_buf,
            pltpu.VMEM((2 * rows, rows_total), BF16),
            pltpu.VMEM((rows_total, 2 * rows), BF16),
            pltpu.VMEM((n, units_per, LANES), F32),
            pltpu.VMEM((n, units_per, LANES), F32),
            pltpu.SemaphoreType.DMA((2,)),
            pltpu.SemaphoreType.DMA((1 + chunks,)),
            pltpu.SemaphoreType.DMA,
            pltpu.SemaphoreType.DMA,
            pltpu.SemaphoreType.DMA((chunks,)),
            pltpu.SemaphoreType.DMA((chunks,)),
            pltpu.SemaphoreType.DMA((chunks,)),
            pltpu.SemaphoreType.DMA((chunks,)),
            pltpu.SemaphoreType.DMA((2,)),
            pltpu.SemaphoreType.DMA((2,)),
        ],
        compiler_params=pltpu.CompilerParams(
            collective_id=0, has_side_effects=True, vmem_limit_bytes=VMEM_LIMIT
        ),
        name="exchange",
    )(
        block_ids,
        slot_mask,
        activations,
        enc_bias.reshape(1, width),
        dec_bias.reshape(1, model_width),
        enc_weight,
        dec_weight,
    )
    tiles = 2
    tile = half // tiles
    grad_enc, grad_dec = pl.pallas_call(
        grad_kernel,
        grid=(2, tiles),
        out_shape=(
            jax.ShapeDtypeStruct((model_width, width), F32),
            jax.ShapeDtypeStruct((width, model_width), F32),
        ),
        in_specs=[
            pl.BlockSpec((rows_total, tile), lambda h, j: (0, j)),
            pl.BlockSpec((rows_total, tile), lambda h, j: (0, j)),
            pl.BlockSpec((rows_total, width), lambda h, j: (0, 0)),
            pl.BlockSpec((rows_total, width), lambda h, j: (0, 0)),
        ],
        out_specs=(
            pl.BlockSpec((tile, width), lambda h, j: (h * tiles + j, 0)),
            pl.BlockSpec((width, tile), lambda h, j: (0, h * tiles + j)),
        ),
        compiler_params=pltpu.CompilerParams(vmem_limit_bytes=VMEM_LIMIT),
        name="grads",
    )(rows_in, err_in, latent, dlatent)
    return (
        recon_error,
        grad_enc,
        enc_bias_grad.reshape(width),
        grad_dec,
        sums.reshape(n * units_per * LANES)[:model_width],
    )


def solution(mesh):
    return jax.shard_map(
        body,
        mesh=mesh,
        in_specs=(
            P(("groups", "dict"), None),
            P(("groups", "dict"), None),
            P(("groups", "dict"), None),
            P(None, "dict"),
            P("dict"),
            P("dict", None),
            P(),
        ),
        out_specs=(
            P(("groups", "dict"), None),
            P("groups", "dict"),
            P(("groups", "dict")),
            P(("groups", "dict"), None),
            P("groups"),
        ),
        check_vma=False,
    )
```

```python
import functools

import jax
import jax.numpy as jnp
from jax import lax
from jax.experimental import pallas as pl
from jax.experimental.pallas import tpu as pltpu
from jax.sharding import PartitionSpec as P

BLOCK = 64
CAP = 2
ROW_DEV = 128
SCALE = 1.0 / ROW_DEV
LANES = 128
TILES = 2
VMEM_LIMIT = 58 * 1024 * 1024
F32 = jnp.float32
BF16 = jnp.bfloat16


def chunk_list(half):
    units = half // LANES
    parts = [4, 4, 4] if units > 12 else []
    rest = units - sum(parts)
    parts = ([rest] if rest else []) + parts
    out, start = [], 0
    for part in parts:
        out.append((start * LANES, part * LANES))
        start += part
    return out


def dot(a, b):
    return jnp.dot(a, b, preferred_element_type=F32)


def dot_nt(a, b):
    return lax.dot_general(a, b, (((1,), (1,)), ((), ())), preferred_element_type=F32)


def dot_tn(a, b):
    return lax.dot_general(a, b, (((0,), (0,)), ((), ())), preferred_element_type=F32)


def exchange_kernel(
    n, ids_ref, live_ref, enc_bias_ref, dec_bias_ref, act_hbm, enc_hbm, dec_hbm,
    recon_hbm, rows_hbm, err_hbm, lat_ref, dlat_ref, enc_grad_ref, sum_ref,
    act, recon, enc, dec, out_buf, rows_in, term_out, term_in, err_in, pick, pick_t, part, part_in,
    load_sem, store_sem, send1, recv1, send2, recv2, send3, recv3, send4, recv4,
):
    me = lax.axis_index("dict")
    rows_total = 16 * n
    slots = ids_ref.shape[0]
    rows = ids_ref.shape[1]
    half = act.shape[1]
    width = BLOCK * 4
    chunks = chunk_list(half)
    bits = [1 << k for k in range(n.bit_length() - 1)]

    def peer_of(step):
        index = n - step
        return sum(((me // bit + index // bit) % 2) * bit for bit in bits)

    def for_peers(fn, low=1, high=n):
        def step_fn(step, carry):
            fn(peer_of(step))
            return carry

        lax.fori_loop(low, high, step_fn, 0)

    quarter = n // 4
    mine_quarter = me // quarter
    groups = [
        ((3 - mine_quarter) * quarter, quarter, 1, quarter + 1),
        (((mine_quarter + 2) % 4) * quarter, quarter, quarter + 1, 2 * quarter + 1),
        ((me // (2 * quarter)) * 2 * quarter, 2 * quarter, 2 * quarter + 1, n),
    ]

    act_low = pltpu.make_async_copy(
        act_hbm.at[:, pl.ds(0, half)], act.at[pl.ds(0, rows)], load_sem.at[2]
    )
    act_high = pltpu.make_async_copy(
        act_hbm.at[:, pl.ds(half, half)], act.at[pl.ds(rows, rows)], load_sem.at[3]
    )
    enc_load = pltpu.make_async_copy(enc_hbm, enc, load_sem.at[0])
    dec_load = pltpu.make_async_copy(dec_hbm, dec, load_sem.at[1])
    act_low.start()
    act_high.start()
    enc_load.start()
    dec_load.start()
    barrier = pltpu.get_barrier_semaphore()
    for_peers(
        lambda peer: pl.semaphore_signal(
            barrier, inc=1, device_id={"dict": peer}, device_id_type=pl.DeviceIdType.MESH
        )
    )

    def block_rows(device, count=1):
        return pl.ds(pl.multiple_of(device * 16, 16), count * 16)

    def send(src, dst, start, size, send_sem, recv_sem, low=1, high=n):
        mine = block_rows(me)
        columns = pl.ds(start, size)

        def one(peer):
            pltpu.make_async_remote_copy(
                src_ref=src.at[block_rows(peer), columns],
                dst_ref=dst.at[mine, columns],
                send_sem=send_sem,
                recv_sem=recv_sem,
                device_id={"dict": peer},
                device_id_type=pl.DeviceIdType.MESH,
            ).start()

        for_peers(one, low, high)
        if high == n:
            dst[mine, columns] = src[mine, columns]

    def wait_all(buf, start, size, sem, count=n - 1):
        view = buf.at[pl.ds(0, count * 16), pl.ds(start, size)]
        pltpu.make_async_copy(view, view, sem).wait()

    column = lax.broadcasted_iota(jnp.int32, (slots, rows_total), 1)
    block = (column // 16) * 4 + (column % 8) // CAP
    per_slot = 4 * n // slots
    spread = (
        lax.broadcasted_iota(jnp.int32, (slots, rows_total), 0) == block // per_slot
    ).astype(F32).astype(BF16)
    slot_base = lax.broadcasted_iota(jnp.int32, (slots, rows), 0) * per_slot
    code = jnp.where(live_ref[...] == 1, ids_ref[...] - slot_base + 1, 0).astype(F32)
    code = dot_tn(code.astype(BF16), spread)
    column = lax.broadcasted_iota(jnp.int32, (rows, rows_total), 1)
    block = (column // 16) * 4 + (column % 8) // CAP
    hit = code == (block % per_slot + 1).astype(F32)
    lower = (
        lax.broadcasted_iota(jnp.int32, (rows, rows), 1)
        < lax.broadcasted_iota(jnp.int32, (rows, rows), 0)
    ).astype(F32).astype(BF16)
    earlier = dot(lower, hit.astype(F32).astype(BF16))
    chosen = hit & (earlier == (column % CAP).astype(F32))
    top = (column // 8) % 2
    pick_low = jnp.where(chosen & (top == 0), 1.0, 0.0)
    pick_high = jnp.where(chosen & (top == 1), 1.0, 0.0)
    both = jnp.concatenate([pick_low, pick_high], axis=0)
    pick[...] = both.astype(BF16)
    pick_t[...] = both.T.astype(BF16)
    part[...] = jnp.zeros_like(part)

    act_low.wait()
    act_high.wait()
    for g, (first, count, low, high) in enumerate(groups):
        group_rows = block_rows(first, count)
        for start, size in chunks:
            columns = pl.ds(start, size)
            out_buf[group_rows, columns] = dot(pick_t[group_rows, :], act[:, columns]).astype(BF16)
        if g == 0:
            pl.semaphore_wait(barrier, n - 1)
        send(out_buf, rows_in, 0, half, send1, recv1.at[g], low, high)
    enc_load.wait()
    dec_load.wait()

    def stack(value):
        count = value.shape[0]
        value = jnp.broadcast_to(value[:, None], (count, 2, 8, width))
        return value.reshape(16 * count, width)

    for g, (first, count, low, high) in enumerate(groups):
        group_rows = block_rows(first, count)
        wait_all(rows_in, 0, half, recv1.at[g], count - (1 if high == n else 0))
        value = rows_in[group_rows, :]
        first_half = dot(value, enc[:half, :]).reshape(count, 2, 8, width)
        last_half = dot(value, enc[half:, :]).reshape(count, 2, 8, width)
        preact = first_half[:, 0] + last_half[:, 1] + enc_bias_ref[...].reshape(1, 1, width)
        own_block = (
            lax.broadcasted_iota(jnp.int32, (count, 8, width), 1) // CAP
            == lax.broadcasted_iota(jnp.int32, (count, 8, width), 2) // BLOCK
        )
        latent = stack(jnp.where(own_block, jnp.maximum(preact, 0.0), 0.0))
        lat_ref[group_rows, :] = latent.astype(BF16)
        top = (lax.broadcasted_iota(jnp.int32, latent.shape, 0) // 8) % 2
        latent_low = jnp.where(top == 0, latent, 0.0).astype(BF16)
        latent_high = jnp.where(top == 1, latent, 0.0).astype(BF16)
        for c, (start, size) in enumerate(chunks):
            value = dot(latent_low, dec[:, start : start + size])
            value = value + dot(latent_high, dec[:, half + start : half + start + size])
            term_out[group_rows, start : start + size] = value.astype(BF16)
            send(term_out, term_in, start, size, send2.at[c], recv2.at[c], low, high)

    rows_store = pltpu.make_async_copy(rows_in, rows_hbm, store_sem.at[0])
    rows_store.start()
    wait_all(out_buf, 0, half, send1)

    units_per = part.shape[1]
    for c, (start, size) in enumerate(chunks):
        columns = pl.ds(start, size)
        wait_all(term_in, start, size, recv2.at[c])
        combined = dot(pick[...], term_in[:, columns])
        errors = []
        for h in range(2):
            unit = (h * half + start) // LANES
            bias = jnp.concatenate(
                [dec_bias_ref[unit + u : unit + u + 1, :] for u in range(size // LANES)], axis=1
            )
            residual = combined[h * rows : (h + 1) * rows] + bias
            residual = residual - act[h * rows : (h + 1) * rows, columns].astype(F32)
            errors.append(residual.astype(BF16))
            total = SCALE * jnp.sum(residual, axis=0, keepdims=True)
            for u in range(size // LANES):
                part[(unit + u) // units_per, (unit + u) % units_per, :] = total[
                    0, u * LANES : (u + 1) * LANES
                ]
        error = jnp.concatenate(errors, axis=0)
        recon[:, columns] = error
        out_buf[:, columns] = dot(pick_t[...], error).astype(BF16)
        send(out_buf, err_in, start, size, send3.at[c], recv3.at[c])
    recon_store = pltpu.make_async_copy(recon, recon_hbm, store_sem.at[1])
    recon_store.start()

    def send_part(peer):
        pltpu.make_async_remote_copy(
            src_ref=part.at[peer],
            dst_ref=part_in.at[me],
            send_sem=send4.at[0],
            recv_sem=recv4.at[0],
            device_id={"dict": peer},
            device_id_type=pl.DeviceIdType.MESH,
        ).start()

    for_peers(send_part)
    part_in[me] = part[me]

    def wait_parts(buf, sem):
        view = buf.at[pl.ds(0, n - 1)]
        pltpu.make_async_copy(view, view, sem).wait()

    def send_total(peer):
        pltpu.make_async_remote_copy(
            src_ref=sum_ref.at[me],
            dst_ref=sum_ref.at[me],
            send_sem=send4.at[1],
            recv_sem=recv4.at[1],
            device_id={"dict": peer},
            device_id_type=pl.DeviceIdType.MESH,
        ).start()

    first_half = jnp.zeros((rows_total, width), F32)
    last_half = jnp.zeros((rows_total, width), F32)
    stores = []
    for c, (start, size) in enumerate(chunks):
        if c == len(chunks) - 1:
            wait_parts(part_in, recv4.at[0])
            wait_parts(part, send4.at[0])
            sum_ref[me] = jnp.sum(part_in[...], axis=0)
            for_peers(send_total)
        wait_all(err_in, start, size, recv3.at[c])
        columns = pl.ds(start, size)
        store = pltpu.make_async_copy(
            err_in.at[:, columns], err_hbm.at[:, columns], store_sem.at[2 + c]
        )
        store.start()
        stores.append(store)
        value = err_in[:, columns]
        first_half = first_half + dot_nt(value, dec[:, start : start + size])
        last_half = last_half + dot_nt(value, dec[:, half + start : half + start + size])
    first_half = first_half.reshape(n, 2, 8, width)
    last_half = last_half.reshape(n, 2, 8, width)
    latent = lat_ref[...].astype(F32).reshape(n, 2, 8, width)[:, 0]
    dlatent = jnp.where(latent > 0, SCALE * (first_half[:, 0] + last_half[:, 1]), 0.0)
    enc_grad_ref[...] = jnp.sum(dlatent.reshape(n * 8, width), axis=0, keepdims=True)
    dlat_ref[...] = stack(dlatent).astype(BF16)

    for c, (start, size) in enumerate(chunks):
        wait_all(term_out, start, size, send2.at[c])
        wait_all(out_buf, start, size, send3.at[c])
        stores[c].wait()
    rows_store.wait()
    recon_store.wait()
    wait_parts(sum_ref, recv4.at[1])
    wait_parts(sum_ref, send4.at[1])


def grad_kernel(
    rows_ref, err_ref, lat_ref, dlat_ref, recon_ref, bias_ref, sum_ref,
    enc_out, dec_out, recon_out, bias_out, sum_out,
):
    h = pl.program_id(1)

    @pl.when((pl.program_id(0) == 0) & (h == 0))
    def _():
        bias_out[...] = bias_ref[...]
        per = sum_ref.shape[1]
        for unit in range(sum_out.shape[0]):
            sum_out[unit, :] = sum_ref[unit // per, unit % per, :]

    top = (lax.broadcasted_iota(jnp.int32, lat_ref.shape, 0) // 8) % 2
    keep = top == h
    latent = jnp.where(keep, lat_ref[...].astype(F32), 0.0).astype(BF16)
    dlatent = jnp.where(keep, dlat_ref[...].astype(F32), 0.0).astype(BF16)
    enc_out[...] = dot_tn(rows_ref[...], dlatent)
    dec_out[...] = SCALE * dot_tn(latent, err_ref[...])
    recon_out[...] = recon_ref[...]


def body(activations, block_ids, slot_mask, enc_weight, enc_bias, dec_weight, dec_bias):
    n = lax.axis_size("dict")
    rows, model_width = activations.shape
    half = model_width // 2
    width = enc_bias.shape[0]
    rows_total = 16 * n
    units = model_width // LANES
    units_per = -(-units // n)
    chunks = len(chunk_list(half))
    vmem = pl.BlockSpec(memory_space=pltpu.VMEM)
    hbm = pl.BlockSpec(memory_space=pl.ANY)
    slot_buf = pltpu.VMEM((rows_total, half), BF16)
    recon_error, rows_in, err_in, latent, dlatent, enc_bias_grad, sums = pl.pallas_call(
        functools.partial(exchange_kernel, n),
        out_shape=(
            jax.ShapeDtypeStruct((2 * rows, half), BF16),
            jax.ShapeDtypeStruct((rows_total, half), BF16),
            jax.ShapeDtypeStruct((rows_total, half), BF16),
            jax.ShapeDtypeStruct((rows_total, width), BF16),
            jax.ShapeDtypeStruct((rows_total, width), BF16),
            jax.ShapeDtypeStruct((1, width), F32),
            jax.ShapeDtypeStruct((n, units_per, LANES), F32),
        ),
        in_specs=[vmem] * 4 + [hbm] * 3,
        out_specs=(hbm, hbm, hbm, vmem, vmem, vmem, vmem),
        scratch_shapes=[
            pltpu.VMEM((2 * rows, half), BF16),
            pltpu.VMEM((2 * rows, half), BF16),
            pltpu.VMEM((model_width, width), BF16),
            pltpu.VMEM((width, model_width), BF16),
            slot_buf,
            slot_buf,
            slot_buf,
            slot_buf,
            slot_buf,
            pltpu.VMEM((2 * rows, rows_total), BF16),
            pltpu.VMEM((rows_total, 2 * rows), BF16),
            pltpu.VMEM((n, units_per, LANES), F32),
            pltpu.VMEM((n, units_per, LANES), F32),
            pltpu.SemaphoreType.DMA((4,)),
            pltpu.SemaphoreType.DMA((2 + chunks,)),
            pltpu.SemaphoreType.DMA,
            pltpu.SemaphoreType.DMA((3,)),
            pltpu.SemaphoreType.DMA((chunks,)),
            pltpu.SemaphoreType.DMA((chunks,)),
            pltpu.SemaphoreType.DMA((chunks,)),
            pltpu.SemaphoreType.DMA((chunks,)),
            pltpu.SemaphoreType.DMA((2,)),
            pltpu.SemaphoreType.DMA((2,)),
        ],
        compiler_params=pltpu.CompilerParams(
            collective_id=0, has_side_effects=True, vmem_limit_bytes=VMEM_LIMIT
        ),
        name="exchange",
    )(
        block_ids.T,
        slot_mask.T,
        enc_bias.reshape(1, width),
        dec_bias.reshape(units, LANES),
        activations,
        enc_weight,
        dec_weight,
    )
    tiles = TILES
    tile = half // tiles
    grad_enc, grad_dec, recon_error, enc_bias_grad, sums = pl.pallas_call(
        grad_kernel,
        grid=(tiles, 2),
        out_shape=(
            jax.ShapeDtypeStruct((model_width, width), F32),
            jax.ShapeDtypeStruct((width, model_width), F32),
            jax.ShapeDtypeStruct((rows, model_width), BF16),
            jax.ShapeDtypeStruct((1, width), F32),
            jax.ShapeDtypeStruct((units, LANES), F32),
        ),
        in_specs=[
            pl.BlockSpec((rows_total, tile), lambda j, h: (0, j)),
            pl.BlockSpec((rows_total, tile), lambda j, h: (0, j)),
            pl.BlockSpec((rows_total, width), lambda j, h: (0, 0)),
            pl.BlockSpec((rows_total, width), lambda j, h: (0, 0)),
            pl.BlockSpec((rows, tile), lambda j, h: (h, j)),
            pl.BlockSpec((1, width), lambda j, h: (0, 0)),
            pl.BlockSpec((n, units_per, LANES), lambda j, h: (0, 0, 0)),
        ],
        out_specs=(
            pl.BlockSpec((tile, width), lambda j, h: (h * tiles + j, 0)),
            pl.BlockSpec((width, tile), lambda j, h: (0, h * tiles + j)),
            pl.BlockSpec((rows, tile), lambda j, h: (0, h * tiles + j)),
            pl.BlockSpec((1, width), lambda j, h: (0, 0)),
            pl.BlockSpec((units, LANES), lambda j, h: (0, 0)),
        ),
        compiler_params=pltpu.CompilerParams(vmem_limit_bytes=VMEM_LIMIT),
        name="grads",
    )(rows_in, err_in, latent, dlatent, recon_error, enc_bias_grad, sums)
    return (
        recon_error,
        grad_enc,
        enc_bias_grad.reshape(width),
        grad_dec,
        sums.reshape(model_width),
    )


def solution(mesh):
    return jax.shard_map(
        body,
        mesh=mesh,
        in_specs=(
            P(("groups", "dict"), None),
            P(("groups", "dict"), None),
            P(("groups", "dict"), None),
            P(None, "dict"),
            P("dict"),
            P("dict", None),
            P(),
        ),
        out_specs=(
            P(("groups", "dict"), None),
            P("groups", "dict"),
            P(("groups", "dict")),
            P(("groups", "dict"), None),
            P("groups"),
        ),
        check_vma=False,
    )
```

```python
import functools

import jax
import jax.numpy as jnp
from jax import lax
from jax.experimental import pallas as pl
from jax.experimental.pallas import tpu as pltpu
from jax.sharding import PartitionSpec as P

BLOCK = 64
CAP = 2
ROW_DEV = 128
SCALE = 1.0 / ROW_DEV
LANES = 128
TILES = 2
VMEM_LIMIT = 58 * 1024 * 1024
F32 = jnp.float32
BF16 = jnp.bfloat16


def chunk_list(half):
    units = half // LANES
    parts = [4, 4, 4] if units > 12 else []
    rest = units - sum(parts)
    parts = ([rest] if rest else []) + parts
    out, start = [], 0
    for part in parts:
        out.append((start * LANES, part * LANES))
        start += part
    return out


def dot(a, b):
    return jnp.dot(a, b, preferred_element_type=F32)


def dot_nt(a, b):
    return lax.dot_general(a, b, (((1,), (1,)), ((), ())), preferred_element_type=F32)


def dot_tn(a, b):
    return lax.dot_general(a, b, (((0,), (0,)), ((), ())), preferred_element_type=F32)


def exchange_kernel(
    n, ids_ref, live_ref, enc_bias_ref, dec_bias_ref, act_hbm, enc_hbm, dec_hbm,
    recon_hbm, rows_hbm, err_hbm, lat_ref, dlat_ref, enc_grad_ref, sum_ref,
    act, recon, enc, dec, out_buf, rows_in, term_out, term_in, err_in, pick, pick_t, part, part_in,
    load_sem, store_sem, send1, recv1, send2, recv2, send3, recv3, send4, recv4,
):
    me = lax.axis_index("dict")
    rows_total = 16 * n
    slots = ids_ref.shape[0]
    rows = ids_ref.shape[1]
    half = act.shape[1]
    width = BLOCK * 4
    chunks = chunk_list(half)
    bits = [1 << k for k in range(n.bit_length() - 1)]

    def peer_of(step):
        index = n - step
        return sum(((me // bit + index // bit) % 2) * bit for bit in bits)

    def for_peers(fn, low=1, high=n):
        def step_fn(step, carry):
            fn(peer_of(step))
            return carry

        lax.fori_loop(low, high, step_fn, 0)

    quarter = n // 4
    mine_quarter = me // quarter
    groups = [
        ((3 - mine_quarter) * quarter, quarter, 1, quarter + 1),
        (((mine_quarter + 2) % 4) * quarter, quarter, quarter + 1, 2 * quarter + 1),
        ((me // (2 * quarter)) * 2 * quarter, 2 * quarter, 2 * quarter + 1, n),
    ]

    act_low = pltpu.make_async_copy(
        act_hbm.at[:, pl.ds(0, half)], act.at[pl.ds(0, rows)], load_sem.at[2]
    )
    act_high = pltpu.make_async_copy(
        act_hbm.at[:, pl.ds(half, half)], act.at[pl.ds(rows, rows)], load_sem.at[3]
    )
    enc_load = pltpu.make_async_copy(enc_hbm, enc, load_sem.at[0])
    dec_load = pltpu.make_async_copy(dec_hbm, dec, load_sem.at[1])
    act_low.start()
    act_high.start()
    barrier = pltpu.get_barrier_semaphore()
    for_peers(
        lambda peer: pl.semaphore_signal(
            barrier, inc=1, device_id={"dict": peer}, device_id_type=pl.DeviceIdType.MESH
        )
    )

    def block_rows(device, count=1):
        return pl.ds(pl.multiple_of(device * 16, 16), count * 16)

    def send(src, dst, start, size, send_sem, recv_sem, low=1, high=n):
        mine = block_rows(me)
        columns = pl.ds(start, size)

        def one(peer):
            pltpu.make_async_remote_copy(
                src_ref=src.at[block_rows(peer), columns],
                dst_ref=dst.at[mine, columns],
                send_sem=send_sem,
                recv_sem=recv_sem,
                device_id={"dict": peer},
                device_id_type=pl.DeviceIdType.MESH,
            ).start()

        for_peers(one, low, high)
        if high == n:
            dst[mine, columns] = src[mine, columns]

    def wait_all(buf, start, size, sem, count=n - 1):
        view = buf.at[pl.ds(0, count * 16), pl.ds(start, size)]
        pltpu.make_async_copy(view, view, sem).wait()

    column = lax.broadcasted_iota(jnp.int32, (slots, rows_total), 1)
    block = (column // 16) * 4 + (column % 8) // CAP
    per_slot = 4 * n // slots
    spread = (
        lax.broadcasted_iota(jnp.int32, (slots, rows_total), 0) == block // per_slot
    ).astype(F32).astype(BF16)
    slot_base = lax.broadcasted_iota(jnp.int32, (slots, rows), 0) * per_slot
    code = jnp.where(live_ref[...] == 1, ids_ref[...] - slot_base + 1, 0).astype(F32)
    code = dot_tn(code.astype(BF16), spread)
    column = lax.broadcasted_iota(jnp.int32, (rows, rows_total), 1)
    block = (column // 16) * 4 + (column % 8) // CAP
    hit = code == (block % per_slot + 1).astype(F32)
    lower = (
        lax.broadcasted_iota(jnp.int32, (rows, rows), 1)
        < lax.broadcasted_iota(jnp.int32, (rows, rows), 0)
    ).astype(F32).astype(BF16)
    earlier = dot(lower, hit.astype(F32).astype(BF16))
    chosen = hit & (earlier == (column % CAP).astype(F32))
    top = (column // 8) % 2
    pick_low = jnp.where(chosen & (top == 0), 1.0, 0.0)
    pick_high = jnp.where(chosen & (top == 1), 1.0, 0.0)
    both = jnp.concatenate([pick_low, pick_high], axis=0)
    pick[...] = both.astype(BF16)
    pick_t[...] = both.T.astype(BF16)
    part[...] = jnp.zeros_like(part)

    act_low.wait()
    act_high.wait()
    enc_load.start()
    dec_load.start()
    for g, (first, count, low, high) in enumerate(groups):
        group_rows = block_rows(first, count)
        for start, size in chunks:
            columns = pl.ds(start, size)
            out_buf[group_rows, columns] = dot(pick_t[group_rows, :], act[:, columns]).astype(BF16)
        if g == 0:
            pl.semaphore_wait(barrier, n - 1)
        send(out_buf, rows_in, 0, half, send1, recv1.at[g], low, high)
    enc_load.wait()
    dec_load.wait()

    def stack(value):
        count = value.shape[0]
        value = jnp.broadcast_to(value[:, None], (count, 2, 8, width))
        return value.reshape(16 * count, width)

    for g, (first, count, low, high) in enumerate(groups):
        group_rows = block_rows(first, count)
        wait_all(rows_in, 0, half, recv1.at[g], count - (1 if high == n else 0))
        value = rows_in[group_rows, :]
        first_half = dot(value, enc[:half, :]).reshape(count, 2, 8, width)
        last_half = dot(value, enc[half:, :]).reshape(count, 2, 8, width)
        preact = first_half[:, 0] + last_half[:, 1] + enc_bias_ref[...].reshape(1, 1, width)
        own_block = (
            lax.broadcasted_iota(jnp.int32, (count, 8, width), 1) // CAP
            == lax.broadcasted_iota(jnp.int32, (count, 8, width), 2) // BLOCK
        )
        latent = stack(jnp.where(own_block, jnp.maximum(preact, 0.0), 0.0))
        lat_ref[group_rows, :] = latent.astype(BF16)
        top = (lax.broadcasted_iota(jnp.int32, latent.shape, 0) // 8) % 2
        latent_low = jnp.where(top == 0, latent, 0.0).astype(BF16)
        latent_high = jnp.where(top == 1, latent, 0.0).astype(BF16)
        for c, (start, size) in enumerate(chunks):
            value = dot(latent_low, dec[:, start : start + size])
            value = value + dot(latent_high, dec[:, half + start : half + start + size])
            term_out[group_rows, start : start + size] = value.astype(BF16)
            send(term_out, term_in, start, size, send2.at[c], recv2.at[c], low, high)

    rows_store = pltpu.make_async_copy(rows_in, rows_hbm, store_sem.at[0])
    rows_store.start()
    wait_all(out_buf, 0, half, send1)

    def send_part(peer):
        pltpu.make_async_remote_copy(
            src_ref=part.at[peer],
            dst_ref=part_in.at[me],
            send_sem=send4.at[0],
            recv_sem=recv4.at[0],
            device_id={"dict": peer},
            device_id_type=pl.DeviceIdType.MESH,
        ).start()

    units_per = part.shape[1]
    for c, (start, size) in enumerate(chunks):
        columns = pl.ds(start, size)
        wait_all(term_in, start, size, recv2.at[c])
        combined = dot(pick[...], term_in[:, columns])
        errors = []
        for h in range(2):
            unit = (h * half + start) // LANES
            bias = jnp.concatenate(
                [dec_bias_ref[unit + u : unit + u + 1, :] for u in range(size // LANES)], axis=1
            )
            residual = combined[h * rows : (h + 1) * rows] + bias
            residual = residual - act[h * rows : (h + 1) * rows, columns].astype(F32)
            errors.append(residual.astype(BF16))
            total = SCALE * jnp.sum(residual, axis=0, keepdims=True)
            for u in range(size // LANES):
                part[(unit + u) // units_per, (unit + u) % units_per, :] = total[
                    0, u * LANES : (u + 1) * LANES
                ]
        if c == len(chunks) - 1:
            for_peers(send_part)
            part_in[me] = part[me]
        error = jnp.concatenate(errors, axis=0)
        recon[:, columns] = error
        out_buf[:, columns] = dot(pick_t[...], error).astype(BF16)
        send(out_buf, err_in, start, size, send3.at[c], recv3.at[c])
    recon_store = pltpu.make_async_copy(recon, recon_hbm, store_sem.at[1])
    recon_store.start()

    def wait_parts(buf, sem):
        view = buf.at[pl.ds(0, n - 1)]
        pltpu.make_async_copy(view, view, sem).wait()

    def send_total(peer):
        pltpu.make_async_remote_copy(
            src_ref=sum_ref.at[me],
            dst_ref=sum_ref.at[me],
            send_sem=send4.at[1],
            recv_sem=recv4.at[1],
            device_id={"dict": peer},
            device_id_type=pl.DeviceIdType.MESH,
        ).start()

    first_half = jnp.zeros((rows_total, width), F32)
    last_half = jnp.zeros((rows_total, width), F32)
    stores = []
    for c, (start, size) in enumerate(chunks):
        if c == len(chunks) - 1:
            wait_parts(part_in, recv4.at[0])
            wait_parts(part, send4.at[0])
            sum_ref[me] = jnp.sum(part_in[...], axis=0)
            for_peers(send_total)
        wait_all(err_in, start, size, recv3.at[c])
        columns = pl.ds(start, size)
        store = pltpu.make_async_copy(
            err_in.at[:, columns], err_hbm.at[:, columns], store_sem.at[2 + c]
        )
        store.start()
        stores.append(store)
        value = err_in[:, columns]
        first_half = first_half + dot_nt(value, dec[:, start : start + size])
        last_half = last_half + dot_nt(value, dec[:, half + start : half + start + size])
    first_half = first_half.reshape(n, 2, 8, width)
    last_half = last_half.reshape(n, 2, 8, width)
    latent = lat_ref[...].astype(F32).reshape(n, 2, 8, width)[:, 0]
    dlatent = jnp.where(latent > 0, SCALE * (first_half[:, 0] + last_half[:, 1]), 0.0)
    enc_grad_ref[...] = jnp.sum(dlatent.reshape(n * 8, width), axis=0, keepdims=True)
    dlat_ref[...] = stack(dlatent).astype(BF16)

    for c, (start, size) in enumerate(chunks):
        wait_all(term_out, start, size, send2.at[c])
        wait_all(out_buf, start, size, send3.at[c])
        stores[c].wait()
    rows_store.wait()
    recon_store.wait()
    wait_parts(sum_ref, recv4.at[1])
    wait_parts(sum_ref, send4.at[1])


def grad_kernel(
    rows_ref, err_ref, lat_ref, dlat_ref, recon_ref, bias_ref, sum_ref,
    enc_out, dec_out, recon_out, bias_out, sum_out,
):
    h = pl.program_id(1)

    @pl.when((pl.program_id(0) == 0) & (h == 0))
    def _():
        bias_out[...] = bias_ref[...]
        per = sum_ref.shape[1]
        for unit in range(sum_out.shape[0]):
            sum_out[unit, :] = sum_ref[unit // per, unit % per, :]

    top = (lax.broadcasted_iota(jnp.int32, lat_ref.shape, 0) // 8) % 2
    keep = top == h
    latent = jnp.where(keep, lat_ref[...].astype(F32), 0.0).astype(BF16)
    dlatent = jnp.where(keep, dlat_ref[...].astype(F32), 0.0).astype(BF16)
    enc_out[...] = dot_tn(rows_ref[...], dlatent)
    dec_out[...] = SCALE * dot_tn(latent, err_ref[...])
    recon_out[...] = recon_ref[...]


def body(activations, block_ids, slot_mask, enc_weight, enc_bias, dec_weight, dec_bias):
    n = lax.axis_size("dict")
    rows, model_width = activations.shape
    half = model_width // 2
    width = enc_bias.shape[0]
    rows_total = 16 * n
    units = model_width // LANES
    units_per = -(-units // n)
    chunks = len(chunk_list(half))
    vmem = pl.BlockSpec(memory_space=pltpu.VMEM)
    hbm = pl.BlockSpec(memory_space=pl.ANY)
    slot_buf = pltpu.VMEM((rows_total, half), BF16)
    recon_error, rows_in, err_in, latent, dlatent, enc_bias_grad, sums = pl.pallas_call(
        functools.partial(exchange_kernel, n),
        out_shape=(
            jax.ShapeDtypeStruct((2 * rows, half), BF16),
            jax.ShapeDtypeStruct((rows_total, half), BF16),
            jax.ShapeDtypeStruct((rows_total, half), BF16),
            jax.ShapeDtypeStruct((rows_total, width), BF16),
            jax.ShapeDtypeStruct((rows_total, width), BF16),
            jax.ShapeDtypeStruct((1, width), F32),
            jax.ShapeDtypeStruct((n, units_per, LANES), F32),
        ),
        in_specs=[vmem] * 4 + [hbm] * 3,
        out_specs=(hbm, hbm, hbm, vmem, vmem, vmem, vmem),
        scratch_shapes=[
            pltpu.VMEM((2 * rows, half), BF16),
            pltpu.VMEM((2 * rows, half), BF16),
            pltpu.VMEM((model_width, width), BF16),
            pltpu.VMEM((width, model_width), BF16),
            slot_buf,
            slot_buf,
            slot_buf,
            slot_buf,
            slot_buf,
            pltpu.VMEM((2 * rows, rows_total), BF16),
            pltpu.VMEM((rows_total, 2 * rows), BF16),
            pltpu.VMEM((n, units_per, LANES), F32),
            pltpu.VMEM((n, units_per, LANES), F32),
            pltpu.SemaphoreType.DMA((4,)),
            pltpu.SemaphoreType.DMA((2 + chunks,)),
            pltpu.SemaphoreType.DMA,
            pltpu.SemaphoreType.DMA((3,)),
            pltpu.SemaphoreType.DMA((chunks,)),
            pltpu.SemaphoreType.DMA((chunks,)),
            pltpu.SemaphoreType.DMA((chunks,)),
            pltpu.SemaphoreType.DMA((chunks,)),
            pltpu.SemaphoreType.DMA((2,)),
            pltpu.SemaphoreType.DMA((2,)),
        ],
        compiler_params=pltpu.CompilerParams(
            collective_id=0, has_side_effects=True, vmem_limit_bytes=VMEM_LIMIT
        ),
        name="exchange",
    )(
        block_ids.T,
        slot_mask.T,
        enc_bias.reshape(1, width),
        dec_bias.reshape(units, LANES),
        activations,
        enc_weight,
        dec_weight,
    )
    tiles = TILES
    tile = half // tiles
    grad_enc, grad_dec, recon_error, enc_bias_grad, sums = pl.pallas_call(
        grad_kernel,
        grid=(tiles, 2),
        out_shape=(
            jax.ShapeDtypeStruct((model_width, width), F32),
            jax.ShapeDtypeStruct((width, model_width), F32),
            jax.ShapeDtypeStruct((rows, model_width), BF16),
            jax.ShapeDtypeStruct((1, width), F32),
            jax.ShapeDtypeStruct((units, LANES), F32),
        ),
        in_specs=[
            pl.BlockSpec((rows_total, tile), lambda j, h: (0, j)),
            pl.BlockSpec((rows_total, tile), lambda j, h: (0, j)),
            pl.BlockSpec((rows_total, width), lambda j, h: (0, 0)),
            pl.BlockSpec((rows_total, width), lambda j, h: (0, 0)),
            pl.BlockSpec((rows, tile), lambda j, h: (h, j)),
            pl.BlockSpec((1, width), lambda j, h: (0, 0)),
            pl.BlockSpec((n, units_per, LANES), lambda j, h: (0, 0, 0)),
        ],
        out_specs=(
            pl.BlockSpec((tile, width), lambda j, h: (h * tiles + j, 0)),
            pl.BlockSpec((width, tile), lambda j, h: (0, h * tiles + j)),
            pl.BlockSpec((rows, tile), lambda j, h: (0, h * tiles + j)),
            pl.BlockSpec((1, width), lambda j, h: (0, 0)),
            pl.BlockSpec((units, LANES), lambda j, h: (0, 0)),
        ),
        compiler_params=pltpu.CompilerParams(vmem_limit_bytes=VMEM_LIMIT),
        name="grads",
    )(rows_in, err_in, latent, dlatent, recon_error, enc_bias_grad, sums)
    return (
        recon_error,
        grad_enc,
        enc_bias_grad.reshape(width),
        grad_dec,
        sums.reshape(model_width),
    )


def solution(mesh):
    return jax.shard_map(
        body,
        mesh=mesh,
        in_specs=(
            P(("groups", "dict"), None),
            P(("groups", "dict"), None),
            P(("groups", "dict"), None),
            P(None, "dict"),
            P("dict"),
            P("dict", None),
            P(),
        ),
        out_specs=(
            P(("groups", "dict"), None),
            P("groups", "dict"),
            P(("groups", "dict")),
            P(("groups", "dict"), None),
            P("groups"),
        ),
        check_vma=False,
    )
```

```python
import functools

import jax
import jax.numpy as jnp
from jax import lax
from jax.experimental import pallas as pl
from jax.experimental.pallas import tpu as pltpu
from jax.sharding import PartitionSpec as P

BLOCK = 64
CAP = 2
ROW_DEV = 128
SCALE = 1.0 / ROW_DEV
LANES = 128
TILES = 1
VMEM_LIMIT = 58 * 1024 * 1024
F32 = jnp.float32
BF16 = jnp.bfloat16


def chunk_list(half):
    units = half // LANES
    parts = [5, 5] if units > 12 else []
    rest = units - sum(parts)
    parts = ([rest] if rest else []) + parts
    out, start = [], 0
    for part in parts:
        out.append((start * LANES, part * LANES))
        start += part
    return out


def dot(a, b):
    return jnp.dot(a, b, preferred_element_type=F32)


def dot_nt(a, b):
    return lax.dot_general(a, b, (((1,), (1,)), ((), ())), preferred_element_type=F32)


def dot_tn(a, b):
    return lax.dot_general(a, b, (((0,), (0,)), ((), ())), preferred_element_type=F32)


def exchange_kernel(
    n, ids_ref, live_ref, enc_bias_ref, dec_bias_ref, act_hbm, enc_hbm, dec_hbm,
    recon_hbm, rows_hbm, err_hbm, lat_ref, dlat_ref, enc_grad_ref, sum_ref,
    act, recon, enc, dec, out_buf, rows_in, term_out, term_in, err_in, pick, pick_t, part, part_in,
    load_sem, store_sem, send1, recv1, send2, recv2, send3, recv3, send4, recv4,
):
    me = lax.axis_index("dict")
    rows_total = 16 * n
    slots = ids_ref.shape[0]
    rows = ids_ref.shape[1]
    half = act.shape[1]
    width = BLOCK * 4
    chunks = chunk_list(half)
    bits = [1 << k for k in range(n.bit_length() - 1)]

    def peer_of(step):
        index = n - step
        return sum(((me // bit + index // bit) % 2) * bit for bit in bits)

    def for_peers(fn, low=1, high=n):
        def step_fn(step, carry):
            fn(peer_of(step))
            return carry

        lax.fori_loop(low, high, step_fn, 0)

    quarter = n // 4
    mine_quarter = me // quarter
    groups = [
        ((3 - mine_quarter) * quarter, quarter, 1, quarter + 1),
        (((mine_quarter + 2) % 4) * quarter, quarter, quarter + 1, 2 * quarter + 1),
        ((me // (2 * quarter)) * 2 * quarter, 2 * quarter, 2 * quarter + 1, n),
    ]

    act_low = pltpu.make_async_copy(
        act_hbm.at[:, pl.ds(0, half)], act.at[pl.ds(0, rows)], load_sem.at[2]
    )
    act_high = pltpu.make_async_copy(
        act_hbm.at[:, pl.ds(half, half)], act.at[pl.ds(rows, rows)], load_sem.at[3]
    )
    enc_load = pltpu.make_async_copy(enc_hbm, enc, load_sem.at[0])
    dec_load = pltpu.make_async_copy(dec_hbm, dec, load_sem.at[1])
    act_low.start()
    act_high.start()
    barrier = pltpu.get_barrier_semaphore()
    for_peers(
        lambda peer: pl.semaphore_signal(
            barrier, inc=1, device_id={"dict": peer}, device_id_type=pl.DeviceIdType.MESH
        )
    )

    def block_rows(device, count=1):
        return pl.ds(pl.multiple_of(device * 16, 16), count * 16)

    def send(src, dst, start, size, send_sem, recv_sem, low=1, high=n):
        mine = block_rows(me)
        columns = pl.ds(start, size)

        def one(peer):
            pltpu.make_async_remote_copy(
                src_ref=src.at[block_rows(peer), columns],
                dst_ref=dst.at[mine, columns],
                send_sem=send_sem,
                recv_sem=recv_sem,
                device_id={"dict": peer},
                device_id_type=pl.DeviceIdType.MESH,
            ).start()

        for_peers(one, low, high)
        if high == n:
            dst[mine, columns] = src[mine, columns]

    def wait_all(buf, start, size, sem, count=n - 1):
        view = buf.at[pl.ds(0, count * 16), pl.ds(start, size)]
        pltpu.make_async_copy(view, view, sem).wait()

    column = lax.broadcasted_iota(jnp.int32, (slots, rows_total), 1)
    block = (column // 16) * 4 + (column % 8) // CAP
    per_slot = 4 * n // slots
    spread = (
        lax.broadcasted_iota(jnp.int32, (slots, rows_total), 0) == block // per_slot
    ).astype(F32).astype(BF16)
    slot_base = lax.broadcasted_iota(jnp.int32, (slots, rows), 0) * per_slot
    code = jnp.where(live_ref[...] == 1, ids_ref[...] - slot_base + 1, 0).astype(F32)
    code = dot_tn(code.astype(BF16), spread)
    column = lax.broadcasted_iota(jnp.int32, (rows, rows_total), 1)
    block = (column // 16) * 4 + (column % 8) // CAP
    hit = code == (block % per_slot + 1).astype(F32)
    lower = (
        lax.broadcasted_iota(jnp.int32, (rows, rows), 1)
        < lax.broadcasted_iota(jnp.int32, (rows, rows), 0)
    ).astype(F32).astype(BF16)
    earlier = dot(lower, hit.astype(F32).astype(BF16))
    chosen = hit & (earlier == (column % CAP).astype(F32))
    top = (column // 8) % 2
    pick_low = jnp.where(chosen & (top == 0), 1.0, 0.0)
    pick_high = jnp.where(chosen & (top == 1), 1.0, 0.0)
    both = jnp.concatenate([pick_low, pick_high], axis=0)
    pick[...] = both.astype(BF16)
    pick_t[...] = both.T.astype(BF16)
    part[...] = jnp.zeros_like(part)

    act_low.wait()
    act_high.wait()
    enc_load.start()
    dec_load.start()
    for g, (first, count, low, high) in enumerate(groups):
        group_rows = block_rows(first, count)
        for start, size in chunks:
            columns = pl.ds(start, size)
            out_buf[group_rows, columns] = dot(pick_t[group_rows, :], act[:, columns]).astype(BF16)
        if g == 0:
            pl.semaphore_wait(barrier, n - 1)
        send(out_buf, rows_in, 0, half, send1, recv1.at[g], low, high)
    enc_load.wait()
    dec_load.wait()

    def stack(value):
        count = value.shape[0]
        value = jnp.broadcast_to(value[:, None], (count, 2, 8, width))
        return value.reshape(16 * count, width)

    for g, (first, count, low, high) in enumerate(groups):
        group_rows = block_rows(first, count)
        wait_all(rows_in, 0, half, recv1.at[g], count - (1 if high == n else 0))
        value = rows_in[group_rows, :]
        first_half = dot(value, enc[:half, :]).reshape(count, 2, 8, width)
        last_half = dot(value, enc[half:, :]).reshape(count, 2, 8, width)
        preact = first_half[:, 0] + last_half[:, 1] + enc_bias_ref[...].reshape(1, 1, width)
        own_block = (
            lax.broadcasted_iota(jnp.int32, (count, 8, width), 1) // CAP
            == lax.broadcasted_iota(jnp.int32, (count, 8, width), 2) // BLOCK
        )
        latent = stack(jnp.where(own_block, jnp.maximum(preact, 0.0), 0.0))
        lat_ref[group_rows, :] = latent.astype(BF16)
        top = (lax.broadcasted_iota(jnp.int32, latent.shape, 0) // 8) % 2
        latent_low = jnp.where(top == 0, latent, 0.0).astype(BF16)
        latent_high = jnp.where(top == 1, latent, 0.0).astype(BF16)
        for c, (start, size) in enumerate(chunks):
            value = dot(latent_low, dec[:, start : start + size])
            value = value + dot(latent_high, dec[:, half + start : half + start + size])
            term_out[group_rows, start : start + size] = value.astype(BF16)
            send(term_out, term_in, start, size, send2.at[c], recv2.at[c], low, high)

    rows_store = pltpu.make_async_copy(rows_in, rows_hbm, store_sem.at[0])
    rows_store.start()
    wait_all(out_buf, 0, half, send1)

    def send_part(peer):
        pltpu.make_async_remote_copy(
            src_ref=part.at[peer],
            dst_ref=part_in.at[me],
            send_sem=send4.at[0],
            recv_sem=recv4.at[0],
            device_id={"dict": peer},
            device_id_type=pl.DeviceIdType.MESH,
        ).start()

    units_per = part.shape[1]
    for c, (start, size) in enumerate(chunks):
        columns = pl.ds(start, size)
        wait_all(term_in, start, size, recv2.at[c])
        combined = dot(pick[...], term_in[:, columns])
        errors = []
        for h in range(2):
            unit = (h * half + start) // LANES
            bias = jnp.concatenate(
                [dec_bias_ref[unit + u : unit + u + 1, :] for u in range(size // LANES)], axis=1
            )
            residual = combined[h * rows : (h + 1) * rows] + bias
            residual = residual - act[h * rows : (h + 1) * rows, columns].astype(F32)
            errors.append(residual.astype(BF16))
            total = SCALE * jnp.sum(residual, axis=0, keepdims=True)
            for u in range(size // LANES):
                part[(unit + u) // units_per, (unit + u) % units_per, :] = total[
                    0, u * LANES : (u + 1) * LANES
                ]
        if c == len(chunks) - 1:
            for_peers(send_part)
            part_in[me] = part[me]
        error = jnp.concatenate(errors, axis=0)
        recon[:, columns] = error
        out_buf[:, columns] = dot(pick_t[...], error).astype(BF16)
        send(out_buf, err_in, start, size, send3.at[c], recv3.at[c])
    recon_store = pltpu.make_async_copy(recon, recon_hbm, store_sem.at[1])
    recon_store.start()

    def wait_parts(buf, sem):
        view = buf.at[pl.ds(0, n - 1)]
        pltpu.make_async_copy(view, view, sem).wait()

    def send_total(peer):
        pltpu.make_async_remote_copy(
            src_ref=sum_ref.at[me],
            dst_ref=sum_ref.at[me],
            send_sem=send4.at[1],
            recv_sem=recv4.at[1],
            device_id={"dict": peer},
            device_id_type=pl.DeviceIdType.MESH,
        ).start()

    first_half = jnp.zeros((rows_total, width), F32)
    last_half = jnp.zeros((rows_total, width), F32)
    stores = []
    for c, (start, size) in enumerate(chunks):
        if c == len(chunks) - 1:
            wait_parts(part_in, recv4.at[0])
            wait_parts(part, send4.at[0])
            sum_ref[me] = jnp.sum(part_in[...], axis=0)
            for_peers(send_total)
        wait_all(err_in, start, size, recv3.at[c])
        columns = pl.ds(start, size)
        store = pltpu.make_async_copy(
            err_in.at[:, columns], err_hbm.at[:, columns], store_sem.at[2 + c]
        )
        store.start()
        stores.append(store)
        value = err_in[:, columns]
        first_half = first_half + dot_nt(value, dec[:, start : start + size])
        last_half = last_half + dot_nt(value, dec[:, half + start : half + start + size])
    first_half = first_half.reshape(n, 2, 8, width)
    last_half = last_half.reshape(n, 2, 8, width)
    latent = lat_ref[...].astype(F32).reshape(n, 2, 8, width)[:, 0]
    dlatent = jnp.where(latent > 0, SCALE * (first_half[:, 0] + last_half[:, 1]), 0.0)
    enc_grad_ref[...] = jnp.sum(dlatent.reshape(n * 8, width), axis=0, keepdims=True)
    dlat_ref[...] = stack(dlatent).astype(BF16)

    for c, (start, size) in enumerate(chunks):
        wait_all(term_out, start, size, send2.at[c])
        wait_all(out_buf, start, size, send3.at[c])
        stores[c].wait()
    rows_store.wait()
    recon_store.wait()
    wait_parts(sum_ref, recv4.at[1])
    wait_parts(sum_ref, send4.at[1])


def grad_kernel(
    rows_ref, err_ref, lat_ref, dlat_ref, recon_ref, bias_ref, sum_ref,
    enc_out, dec_out, recon_out, bias_out, sum_out,
):
    h = pl.program_id(1)

    @pl.when((pl.program_id(0) == 0) & (h == 0))
    def _():
        bias_out[...] = bias_ref[...]
        per = sum_ref.shape[1]
        for unit in range(sum_out.shape[0]):
            sum_out[unit, :] = sum_ref[unit // per, unit % per, :]

    top = (lax.broadcasted_iota(jnp.int32, lat_ref.shape, 0) // 8) % 2
    keep = top == h
    latent = jnp.where(keep, lat_ref[...].astype(F32), 0.0).astype(BF16)
    dlatent = jnp.where(keep, dlat_ref[...].astype(F32), 0.0).astype(BF16)
    enc_out[...] = dot_tn(rows_ref[...], dlatent)
    dec_out[...] = SCALE * dot_tn(latent, err_ref[...])
    recon_out[...] = recon_ref[...]


def body(activations, block_ids, slot_mask, enc_weight, enc_bias, dec_weight, dec_bias):
    n = lax.axis_size("dict")
    rows, model_width = activations.shape
    half = model_width // 2
    width = enc_bias.shape[0]
    rows_total = 16 * n
    units = model_width // LANES
    units_per = -(-units // n)
    chunks = len(chunk_list(half))
    vmem = pl.BlockSpec(memory_space=pltpu.VMEM)
    hbm = pl.BlockSpec(memory_space=pl.ANY)
    slot_buf = pltpu.VMEM((rows_total, half), BF16)
    recon_error, rows_in, err_in, latent, dlatent, enc_bias_grad, sums = pl.pallas_call(
        functools.partial(exchange_kernel, n),
        out_shape=(
            jax.ShapeDtypeStruct((2 * rows, half), BF16),
            jax.ShapeDtypeStruct((rows_total, half), BF16),
            jax.ShapeDtypeStruct((rows_total, half), BF16),
            jax.ShapeDtypeStruct((rows_total, width), BF16),
            jax.ShapeDtypeStruct((rows_total, width), BF16),
            jax.ShapeDtypeStruct((1, width), F32),
            jax.ShapeDtypeStruct((n, units_per, LANES), F32),
        ),
        in_specs=[vmem] * 4 + [hbm] * 3,
        out_specs=(hbm, hbm, hbm, vmem, vmem, vmem, vmem),
        scratch_shapes=[
            pltpu.VMEM((2 * rows, half), BF16),
            pltpu.VMEM((2 * rows, half), BF16),
            pltpu.VMEM((model_width, width), BF16),
            pltpu.VMEM((width, model_width), BF16),
            slot_buf,
            slot_buf,
            slot_buf,
            slot_buf,
            slot_buf,
            pltpu.VMEM((2 * rows, rows_total), BF16),
            pltpu.VMEM((rows_total, 2 * rows), BF16),
            pltpu.VMEM((n, units_per, LANES), F32),
            pltpu.VMEM((n, units_per, LANES), F32),
            pltpu.SemaphoreType.DMA((4,)),
            pltpu.SemaphoreType.DMA((2 + chunks,)),
            pltpu.SemaphoreType.DMA,
            pltpu.SemaphoreType.DMA((3,)),
            pltpu.SemaphoreType.DMA((chunks,)),
            pltpu.SemaphoreType.DMA((chunks,)),
            pltpu.SemaphoreType.DMA((chunks,)),
            pltpu.SemaphoreType.DMA((chunks,)),
            pltpu.SemaphoreType.DMA((2,)),
            pltpu.SemaphoreType.DMA((2,)),
        ],
        compiler_params=pltpu.CompilerParams(
            collective_id=0, has_side_effects=True, vmem_limit_bytes=VMEM_LIMIT
        ),
        name="exchange",
    )(
        block_ids.T,
        slot_mask.T,
        enc_bias.reshape(1, width),
        dec_bias.reshape(units, LANES),
        activations,
        enc_weight,
        dec_weight,
    )
    tiles = TILES
    tile = half // tiles
    grad_enc, grad_dec, recon_error, enc_bias_grad, sums = pl.pallas_call(
        grad_kernel,
        grid=(tiles, 2),
        out_shape=(
            jax.ShapeDtypeStruct((model_width, width), F32),
            jax.ShapeDtypeStruct((width, model_width), F32),
            jax.ShapeDtypeStruct((rows, model_width), BF16),
            jax.ShapeDtypeStruct((1, width), F32),
            jax.ShapeDtypeStruct((units, LANES), F32),
        ),
        in_specs=[
            pl.BlockSpec((rows_total, tile), lambda j, h: (0, j)),
            pl.BlockSpec((rows_total, tile), lambda j, h: (0, j)),
            pl.BlockSpec((rows_total, width), lambda j, h: (0, 0)),
            pl.BlockSpec((rows_total, width), lambda j, h: (0, 0)),
            pl.BlockSpec((rows, tile), lambda j, h: (h, j)),
            pl.BlockSpec((1, width), lambda j, h: (0, 0)),
            pl.BlockSpec((n, units_per, LANES), lambda j, h: (0, 0, 0)),
        ],
        out_specs=(
            pl.BlockSpec((tile, width), lambda j, h: (h * tiles + j, 0)),
            pl.BlockSpec((width, tile), lambda j, h: (0, h * tiles + j)),
            pl.BlockSpec((rows, tile), lambda j, h: (0, h * tiles + j)),
            pl.BlockSpec((1, width), lambda j, h: (0, 0)),
            pl.BlockSpec((units, LANES), lambda j, h: (0, 0)),
        ),
        compiler_params=pltpu.CompilerParams(vmem_limit_bytes=VMEM_LIMIT),
        name="grads",
    )(rows_in, err_in, latent, dlatent, recon_error, enc_bias_grad, sums)
    return (
        recon_error,
        grad_enc,
        enc_bias_grad.reshape(width),
        grad_dec,
        sums.reshape(model_width),
    )


def solution(mesh):
    return jax.shard_map(
        body,
        mesh=mesh,
        in_specs=(
            P(("groups", "dict"), None),
            P(("groups", "dict"), None),
            P(("groups", "dict"), None),
            P(None, "dict"),
            P("dict"),
            P("dict", None),
            P(),
        ),
        out_specs=(
            P(("groups", "dict"), None),
            P("groups", "dict"),
            P(("groups", "dict")),
            P(("groups", "dict"), None),
            P("groups"),
        ),
        check_vma=False,
    )
```
